32 devices in a mesh: section: 4 (over x, core), shard: 8 (over z, y).
Axes of the slice: x: 2, y: 2, z: 4, core: 2. Of those that a mesh axis runs over, the one named last changes fastest.
Arguments:
- features: bfloat16 [2048, 6144], P('shard', 'section'), may hold values from -0.29882812 to 0.29882812
- proj_weight: bfloat16 [6144, 1024], P('section'), may hold values from -0.078125 to 0.078125
- captions: bfloat16 [32, 1024], P('shard'), may hold values from -6 to 6
- positives: int32 [2048], P('shard'), may hold values from 0 to 31
Outputs:
- region_grad: bfloat16 [2048, 6144], P('shard', 'section')
- caption_grad: float32 [32, 1024], P('shard')
The draws below stay inside these ranges and needn't reach their ends.
All inputs are finite; a program needn't handle non-finite values.
Results may differ from the reference program's by a relative error of at most 0.0062.
Values may be sent and summed in bfloat16 or wider, within the bound.
A program may use at most 64 MiB of HBM per device.

```python
import jax
import jax.numpy as jnp
from jax import lax

D = 6144
E = 1024
REGIONS = 2048
CAPTIONS = 32


def with_ends(values, rng, low, largest):
    longest = values.shape.index(max(values.shape))
    spots = []
    for shift in (0, 1):
        where = [jax.random.randint(jax.random.fold_in(rng, axis), (), 0, length) for axis, length in enumerate(values.shape)]
        where[longest] = (where[longest] + shift) % values.shape[longest]
        spots.append(tuple(where))
    return values.at[spots[0]].set(low).at[spots[1]].set(largest)


def block_levels(rng, dims, shards, low, largest):
    gain, own = 1.0, jax.random.fold_in(rng, 6)
    for axis_at, shards_of in shards:
        heights = jnp.exp(jax.random.uniform(jax.random.fold_in(own, axis_at), (shards_of,), jnp.float32, low / len(shards), largest / len(shards)))
        gain = gain * jnp.repeat(heights, dims[axis_at] // shards_of).reshape([-1 if axis == axis_at else 1 for axis in range(len(dims))])
    return gain


def noise(own_key, shape, width, reach, cuts=(), kind=jnp.bfloat16):
    array = width * jax.random.normal(own_key, shape, jnp.float32)
    if cuts:
        array = array * block_levels(own_key, shape, cuts, -0.22, 0.18)
    return jnp.clip(array, -reach, reach).astype(kind)


def setup_inputs(seed: int = 0) -> dict:
    streams_of = jax.random.split(jax.random.key(seed), 5)
    return {
        "features": noise(streams_of[0], (REGIONS, D), 0.05, 0.29882812, ((0, 8), (1, 4))),
        "proj_weight": noise(streams_of[1], (D, E), D ** -0.5, 0.078125, ((0, 4),)),
        "captions": noise(streams_of[2], (CAPTIONS, E), 1.0, 6.0, ((0, 8),)),
        "positives": with_ends(jax.random.randint(streams_of[3], (REGIONS,), 0, CAPTIONS), jax.random.fold_in(streams_of[3], 1), 0, CAPTIONS - 1).astype(jnp.int32),
    }


logit_scale = 14.0
eps_norm = 1e-06

def reference(features, proj_weight, captions, positives):
    projected = jnp.dot(features, proj_weight, preferred_element_type=jnp.float32)
    region_scale = lax.rsqrt(lax.optimization_barrier(jnp.sum(projected * projected, axis=1, keepdims=True)) + eps_norm)
    region_unit = projected * region_scale
    region_half = region_unit.astype(jnp.bfloat16)
    caption_float = captions.astype(jnp.float32)
    caption_scale = lax.rsqrt(lax.optimization_barrier(jnp.sum(caption_float * caption_float, axis=1, keepdims=True)) + eps_norm)
    caption_unit = caption_float * caption_scale
    caption_half = caption_unit.astype(jnp.bfloat16)
    logits = logit_scale * lax.dot_general(region_half, caption_half, (((1,), (1,)), ((), ())), preferred_element_type=jnp.float32)
    expon = jnp.exp(logits)
    probs = expon / lax.optimization_barrier(jnp.sum(expon, axis=1, keepdims=True))
    column_ids = jnp.arange(captions.shape[0], dtype=jnp.int32)
    onehot = (column_ids[None, :] == positives[:, None]).astype(jnp.float32)
    dlogits = (probs - onehot).astype(jnp.bfloat16)
    dunit = logit_scale * jnp.dot(dlogits, caption_half, preferred_element_type=jnp.float32)
    dprojected = (region_scale * (dunit - region_unit * lax.optimization_barrier(jnp.sum(region_unit * dunit, axis=1, keepdims=True)))).astype(jnp.bfloat16)
    region_grad = lax.dot_general(dprojected, proj_weight, (((1,), (1,)), ((), ())), preferred_element_type=jnp.float32).astype(jnp.bfloat16)
    dcaption = logit_scale * lax.dot_general(dlogits, region_half, (((0,), (0,)), ((), ())), preferred_element_type=jnp.float32)
    caption_grad = caption_scale * (dcaption - caption_unit * lax.optimization_barrier(jnp.sum(caption_unit * dcaption, axis=1, keepdims=True)))
    return (region_grad, caption_grad)
```

```python
import functools

import jax
import jax.numpy as jnp
from jax import lax
from jax.experimental import pallas as pl
from jax.experimental.pallas import tpu as pltpu
from jax.sharding import PartitionSpec as P

logit_scale = 14.0
eps_norm = 1e-06
MESH = pl.DeviceIdType.MESH
F32 = jnp.float32
BF16 = jnp.bfloat16
SLOT = 16
CHUNKS = 4
PIECES = 3


def each(low, high, body):
    if high - low <= 8:
        for k in range(low, high):
            body(k)
    else:
        lax.fori_loop(low, high, lambda k, c: (body(k), c)[1], 0)


def kernel(
    sections, shards, f_hbm, w_hbm, cap_ref, pos_ref, rg_hbm, cg_ref,
    fv, wv, own, psnd, prcv, xr, dp, og, cs, tab, dacc, dpt, dsnd, drc,
    f_sem, w_sem, og_sem, ps_sem, pr_sem, xs_sem, xr_sem, ds_sem, dr_sem,
    cs_sem, cr_sem, as_sem, ar_sem, gs_sem, gr_sem,
):
    chips = sections // 2
    n_chunks, _, rows, depth = fv.shape
    width = wv.shape[1]
    half_rows = n_chunks * rows
    caps = cap_ref.shape[0]
    packs = SLOT // caps
    lanes = width // packs
    sec = lax.axis_index("section")
    t = lax.axis_index("shard")
    core = lax.rem(sec, 2)
    chip = sec // 2
    mate = chip * 2 + (1 - core)

    def chip_peer(k):
        return lax.rem(chip + k, chips)

    def shard_peer(k):
        return lax.rem(t + k, shards)

    def place(c, s):
        return {"section": c, "shard": s}

    def row_at(i, which):
        owner = core if which == 1 else 1 - core
        return pl.multiple_of(owner * half_rows + i * rows, rows)

    step = depth // PIECES

    def f_copy(i, which):
        return pltpu.make_async_copy(
            f_hbm.at[pl.ds(row_at(i, which), rows), :], fv.at[i, which], f_sem.at[i, which]
        )

    def w_copy(p):
        band = pl.ds(p * step, step)
        return pltpu.make_async_copy(w_hbm.at[band, :], wv.at[band, :], w_sem.at[p])

    def og_copy(i, which):
        return pltpu.make_async_copy(
            og.at[i, which], rg_hbm.at[pl.ds(row_at(i, which), rows), :], og_sem.at[i, which]
        )

    for which in range(2):
        f_copy(0, which).start()
    for p in range(PIECES):
        w_copy(p).start()
    for i in range(1, n_chunks):
        for which in range(2):
            f_copy(i, which).start()

    barrier = pltpu.get_barrier_semaphore()

    def greet(c, s):
        pl.semaphore_signal(barrier, inc=1, device_id=place(c, s), device_id_type=MESH)

    greet(mate, t)
    each(1, chips, lambda k: greet(chip_peer(k) * 2 + core, t))
    each(1, shards, lambda k: greet(sec, shard_peer(k)))

    cap_float = cap_ref[...].astype(F32)
    cap_scale = lax.rsqrt(jnp.sum(cap_float * cap_float, axis=1, keepdims=True) + eps_norm)
    cap_unit = cap_float * cap_scale
    packed = jnp.concatenate(
        [cap_unit[:, q * lanes : (q + 1) * lanes] for q in range(packs)], axis=0
    )
    cs[t] = packed.astype(BF16)

    pl.semaphore_wait(barrier, 1 + (chips - 1) + (shards - 1))

    def cap_copy(k, source):
        return pltpu.make_async_remote_copy(
            src_ref=cs.at[source], dst_ref=cs.at[source],
            send_sem=cs_sem.at[k], recv_sem=cr_sem.at[source],
            device_id=place(sec, shard_peer(k)), device_id_type=MESH,
        )

    each(1, shards, lambda k: cap_copy(k, t).start())

    def mate_copy(i):
        return pltpu.make_async_remote_copy(
            src_ref=psnd.at[i], dst_ref=prcv.at[i],
            send_sem=ps_sem.at[i], recv_sem=pr_sem.at[i],
            device_id=place(mate, t), device_id_type=MESH,
        )

    def chip_copy(k, i, source):
        return pltpu.make_async_remote_copy(
            src_ref=xr.at[source, i], dst_ref=xr.at[source, i],
            send_sem=xs_sem.at[k, i], recv_sem=xr_sem.at[source, i],
            device_id=place(chip_peer(k) * 2 + core, t), device_id_type=MESH,
        )

    def dp_copy(i):
        return pltpu.make_async_remote_copy(
            src_ref=dp.at[i, 1], dst_ref=dp.at[i, 0],
            send_sem=ds_sem.at[i], recv_sem=dr_sem.at[i],
            device_id=place(mate, t), device_id_type=MESH,
        )

    def chip_sum(i):
        mate_copy(i).wait_recv()
        xr[chip, i] = (own[i] + prcv[i].astype(F32)).astype(BF16)
        each(1, chips, lambda k: chip_copy(k, i, chip).start())

    for i in range(n_chunks):
        for which in range(2):
            f_copy(i, which).wait()
        if i == 0:
            part = None
            for p in range(PIECES):
                w_copy(p).wait()
                band = slice(p * step, (p + 1) * step)
                term = jnp.dot(
                    fv[i, :, :, band].reshape(2 * rows, step), wv[band, :],
                    preferred_element_type=F32,
                )
                part = term if part is None else part + term
        else:
            part = jnp.dot(
                fv[i].reshape(2 * rows, depth), wv[...], preferred_element_type=F32
            )
        psnd[i] = part[:rows].astype(BF16)
        mate_copy(i).start()
        own[i] = part[rows:]
        if i >= 1:
            chip_sum(i - 1)
    chip_sum(n_chunks - 1)

    each(1, shards, lambda k: cap_copy(k, shard_peer(k)).wait_recv())
    per = min(8, shards)
    group = per * SLOT
    ra = lax.broadcasted_iota(jnp.int32, (group, group), 0)
    rb = lax.broadcasted_iota(jnp.int32, (group, group), 1)
    same = jnp.logical_and(ra // SLOT == rb // SLOT, ra % caps == rb % caps)
    picks = [
        jnp.logical_and(same, (rb % SLOT) // caps == q).astype(F32).astype(BF16)
        for q in range(packs)
    ]
    for g in range(shards // per):
        block = cs[g * per : (g + 1) * per].reshape(group, lanes)
        for q in range(packs):
            tab[g * group : (g + 1) * group, q * lanes : (q + 1) * lanes] = jnp.dot(
                picks[q], block, preferred_element_type=F32
            ).astype(BF16)

    positives = pos_ref[...]
    positives = jnp.where(core == 0, positives[:, :half_rows], positives[:, half_rows:])
    total = shards * SLOT
    ids = lax.broadcasted_iota(jnp.int32, (total, rows), 0)
    ids = caps * (ids // SLOT) + ids % caps
    piece = (lax.broadcasted_iota(jnp.int32, (total, lanes), 0) % SLOT) // caps

    def score(i):
        each(1, chips, lambda k: chip_copy(k, i, chip_peer(k)).wait_recv())
        projected = xr[0, i].astype(F32)
        for c in range(1, chips):
            projected = projected + xr[c, i].astype(F32)
        scale = lax.rsqrt(jnp.sum(projected * projected, axis=1, keepdims=True) + eps_norm)
        unit = projected * scale
        half = unit.astype(BF16)
        logits = logit_scale * lax.dot_general(
            tab[...], half, (((1,), (1,)), ((), ())), preferred_element_type=F32
        )
        expon = jnp.exp(logits)
        probs = expon * (packs / jnp.sum(expon, axis=0, keepdims=True))
        onehot = (ids == positives[:, i * rows : (i + 1) * rows]).astype(F32)
        dlogits = (probs - onehot).astype(BF16)
        dunit = (logit_scale / packs) * lax.dot_general(
            dlogits, tab[...], (((0,), (0,)), ((), ())), preferred_element_type=F32
        )
        dproj = scale * (dunit - unit * jnp.sum(unit * dunit, axis=1, keepdims=True))
        dp[i, 1] = dproj.astype(BF16)
        dp_copy(i).start()
        term = jnp.zeros((total, lanes), F32)
        for q in range(packs):
            value = jnp.dot(
                dlogits, half[:, q * lanes : (q + 1) * lanes], preferred_element_type=F32
            )
            term = jnp.where(piece == q, value, term)
        dacc[...] = term if i == 0 else dacc[...] + term

    def grad(i):
        dp_copy(i).wait_recv()
        value = lax.dot_general(
            dp[i].reshape(2 * rows, width), wv[...], (((1,), (1,)), ((), ())),
            preferred_element_type=F32,
        ).astype(BF16)
        og[i] = value.reshape(2, rows, depth)
        for which in range(2):
            og_copy(i, which).start()

    sum_copy = pltpu.make_async_remote_copy(
        src_ref=dacc, dst_ref=dpt, send_sem=as_sem, recv_sem=ar_sem,
        device_id=place(mate, t), device_id_type=MESH,
    )

    def give_copy(k, there, here):
        return pltpu.make_async_remote_copy(
            src_ref=dsnd.at[there], dst_ref=drc.at[here],
            send_sem=gs_sem.at[k], recv_sem=gr_sem.at[here],
            device_id=place(sec, shard_peer(k)), device_id_type=MESH,
        )

    for i in range(n_chunks):
        score(i)
        if i == n_chunks - 1:
            sum_copy.start()
        if i >= 1:
            grad(i - 1)
    sum_copy.wait_recv()
    dsnd[...] = (dacc[...] + dpt[...]).astype(BF16).reshape(shards, SLOT, lanes)
    each(1, shards, lambda k: give_copy(k, shard_peer(k), t).start())
    drc[t] = dsnd[t]
    grad(n_chunks - 1)
    each(1, shards, lambda k: give_copy(k, shard_peer(k), shard_peer(k)).wait_recv())
    dcap = logit_scale * jnp.sum(drc[...].astype(F32), axis=0)
    dcap = jnp.concatenate(
        [dcap[q * caps : (q + 1) * caps, :] for q in range(packs)], axis=1
    )
    cg_ref[...] = cap_scale * (
        dcap - cap_unit * jnp.sum(cap_unit * dcap, axis=1, keepdims=True)
    )

    for i in range(n_chunks):
        for which in range(2):
            og_copy(i, which).wait()
        mate_copy(i).wait_send()
        dp_copy(i).wait_send()
        each(1, chips, lambda k: chip_copy(k, i, chip).wait_send())
    sum_copy.wait_send()
    each(1, shards, lambda k: cap_copy(k, t).wait_send())
    each(1, shards, lambda k: give_copy(k, shard_peer(k), t).wait_send())


def solution(mesh):
    sections, shards = mesh.shape["section"], mesh.shape["shard"]
    chips = sections // 2

    def on_device(features, proj_weight, captions, positives):
        n_rows, depth = features.shape
        width = proj_weight.shape[1]
        caps = captions.shape[0]
        lanes = width * caps // SLOT
        n = CHUNKS
        rows = n_rows // 2 // n
        dma = pltpu.SemaphoreType.DMA
        any_space = pl.BlockSpec(memory_space=pl.ANY)
        vmem = pl.BlockSpec(memory_space=pltpu.VMEM)
        flops = 4 * n_rows * depth * width
        return pl.pallas_call(
            functools.partial(kernel, sections, shards),
            out_shape=(
                jax.ShapeDtypeStruct((n_rows, depth), BF16),
                jax.ShapeDtypeStruct((caps, width), F32),
            ),
            in_specs=[any_space, any_space, vmem, vmem],
            out_specs=(any_space, vmem),
            scratch_shapes=[
                pltpu.VMEM((n, 2, rows, depth), BF16),
                pltpu.VMEM((depth, width), BF16),
                pltpu.VMEM((n, rows, width), F32),
                pltpu.VMEM((n, rows, width), BF16),
                pltpu.VMEM((n, rows, width), BF16),
                pltpu.VMEM((chips, n, rows, width), BF16),
                pltpu.VMEM((n, 2, rows, width), BF16),
                pltpu.VMEM((n, 2, rows, depth), BF16),
                pltpu.VMEM((shards, SLOT, lanes), BF16),
                pltpu.VMEM((shards * SLOT, width), BF16),
                pltpu.VMEM((shards * SLOT, lanes), F32),
                pltpu.VMEM((shards * SLOT, lanes), F32),
                pltpu.VMEM((shards, SLOT, lanes), BF16),
                pltpu.VMEM((shards, SLOT, lanes), BF16),
                dma((n, 2)), dma((PIECES,)), dma((n, 2)),
                dma((n,)), dma((n,)),
                dma((chips, n)), dma((chips, n)),
                dma((n,)), dma((n,)),
                dma((shards,)), dma((shards,)),
                dma, dma,
                dma((shards,)), dma((shards,)),
            ],
            cost_estimate=pl.CostEstimate(
                flops=flops,
                bytes_accessed=2 * (2 * n_rows * depth + depth * width),
                transcendentals=0,
            ),
            compiler_params=pltpu.CompilerParams(
                collective_id=0, has_side_effects=True, vmem_limit_bytes=56 * 1024 * 1024
            ),
        )(features, proj_weight, captions, positives.reshape(1, n_rows))

    return jax.shard_map(
        on_device,
        mesh=mesh,
        in_specs=(P("shard", "section"), P("section", None), P("shard", None), P("shard")),
        out_specs=(P("shard", "section"), P("shard", None)),
        check_vma=False,
    )
```

```python
import functools

import jax
import jax.numpy as jnp
from jax import lax
from jax.experimental import pallas as pl
from jax.experimental.pallas import tpu as pltpu
from jax.sharding import PartitionSpec as P

logit_scale = 14.0
eps_norm = 1e-06
MESH = pl.DeviceIdType.MESH
F32 = jnp.float32
BF16 = jnp.bfloat16
SLOT = 16
CHUNKS = 2
COPIES = 8
PIECES = 3


def each(low, high, body):
    if high - low <= 8:
        for k in range(low, high):
            body(k)
    else:
        lax.fori_loop(low, high, lambda k, c: (body(k), c)[1], 0)


def kernel(
    sections, shards, f_hbm, w_hbm, cap_ref, pos_ref, rg_hbm, cg_ref,
    fv, wv, own, psnd, prcv, xr, dp, og, cs, tab, dacc, dpt, dsnd, drc,
    f_sem, w_sem, og_sem, ps_sem, pr_sem, xs_sem, xr_sem, ds_sem, dr_sem,
    cs_sem, cr_sem, as_sem, ar_sem, gs_sem, gr_sem,
):
    chips = sections // 2
    n_chunks, _, rows, depth = fv.shape
    width = wv.shape[1]
    half_rows = n_chunks * rows
    caps = cap_ref.shape[0]
    packs = SLOT // caps
    lanes = width // packs
    sec = lax.axis_index("section")
    t = lax.axis_index("shard")
    core = lax.rem(sec, 2)
    chip = sec // 2
    mate = chip * 2 + (1 - core)

    def chip_peer(k):
        return lax.rem(chip + k, chips)

    def shard_peer(k):
        return lax.rem(t + k, shards)

    def place(c, s):
        return {"section": c, "shard": s}

    def row_at(i, which):
        owner = core if which == 1 else 1 - core
        return pl.multiple_of(owner * half_rows + i * rows, rows)

    step = depth // PIECES

    def f_copy(i, which):
        return pltpu.make_async_copy(
            f_hbm.at[pl.ds(row_at(i, which), rows), :], fv.at[i, which], f_sem.at[i, which]
        )

    def w_copy(p):
        band = pl.ds(p * step, step)
        return pltpu.make_async_copy(w_hbm.at[band, :], wv.at[band, :], w_sem.at[p])

    def og_copy(i, which):
        return pltpu.make_async_copy(
            og.at[i, which], rg_hbm.at[pl.ds(row_at(i, which), rows), :], og_sem.at[i, which]
        )

    for which in range(2):
        f_copy(0, which).start()
    for p in range(PIECES):
        w_copy(p).start()
    for i in range(1, n_chunks):
        for which in range(2):
            f_copy(i, which).start()

    barrier = pltpu.get_barrier_semaphore()

    def greet(c, s):
        pl.semaphore_signal(barrier, inc=1, device_id=place(c, s), device_id_type=MESH)

    greet(mate, t)
    each(1, chips, lambda k: greet(chip_peer(k) * 2 + core, t))
    each(1, shards, lambda k: greet(sec, shard_peer(k)))

    cap_float = cap_ref[...].astype(F32)
    cap_scale = lax.rsqrt(jnp.sum(cap_float * cap_float, axis=1, keepdims=True) + eps_norm)
    cap_unit = cap_float * cap_scale
    packed = jnp.concatenate(
        [cap_unit[:, q * lanes : (q + 1) * lanes] for q in range(packs)], axis=0
    )
    cs[t] = packed.astype(BF16)

    pl.semaphore_wait(barrier, 1 + (chips - 1) + (shards - 1))

    def cap_copy(k, source):
        return pltpu.make_async_remote_copy(
            src_ref=cs.at[source], dst_ref=cs.at[source],
            send_sem=cs_sem.at[k], recv_sem=cr_sem.at[source],
            device_id=place(sec, shard_peer(k)), device_id_type=MESH,
        )

    each(1, shards, lambda k: cap_copy(k, t).start())

    def mate_copy(i):
        return pltpu.make_async_remote_copy(
            src_ref=psnd.at[i], dst_ref=prcv.at[i],
            send_sem=ps_sem.at[i], recv_sem=pr_sem.at[i],
            device_id=place(mate, t), device_id_type=MESH,
        )

    def chip_copy(k, i, source):
        return pltpu.make_async_remote_copy(
            src_ref=xr.at[source, i], dst_ref=xr.at[source, i],
            send_sem=xs_sem.at[k, i], recv_sem=xr_sem.at[source, i],
            device_id=place(chip_peer(k) * 2 + core, t), device_id_type=MESH,
        )

    def dp_copy(i):
        return pltpu.make_async_remote_copy(
            src_ref=dp.at[i, 1], dst_ref=dp.at[i, 0],
            send_sem=ds_sem.at[i], recv_sem=dr_sem.at[i],
            device_id=place(mate, t), device_id_type=MESH,
        )

    def chip_sum(i):
        mate_copy(i).wait_recv()
        xr[chip, i] = (own[i] + prcv[i].astype(F32)).astype(BF16)
        each(1, chips, lambda k: chip_copy(k, i, chip).start())

    for i in range(n_chunks):
        for which in range(2):
            f_copy(i, which).wait()
        if i == 0:
            part = None
            for p in range(PIECES):
                w_copy(p).wait()
                band = slice(p * step, (p + 1) * step)
                term = jnp.dot(
                    fv[i, :, :, band].reshape(2 * rows, step), wv[band, :],
                    preferred_element_type=F32,
                )
                part = term if part is None else part + term
        else:
            part = jnp.dot(
                fv[i].reshape(2 * rows, depth), wv[...], preferred_element_type=F32
            )
        psnd[i] = part[:rows].astype(BF16)
        mate_copy(i).start()
        own[i] = part[rows:]
        if i >= 1:
            chip_sum(i - 1)
    chip_sum(n_chunks - 1)

    each(1, shards, lambda k: cap_copy(k, shard_peer(k)).wait_recv())
    per = min(8, shards)
    group = per * SLOT
    ra = lax.broadcasted_iota(jnp.int32, (group, group), 0)
    rb = lax.broadcasted_iota(jnp.int32, (group, group), 1)
    same = jnp.logical_and(ra // SLOT == rb // SLOT, ra % caps == rb % caps)
    picks = [
        jnp.logical_and(same, (rb % SLOT) // caps == q).astype(F32).astype(BF16)
        for q in range(packs)
    ]
    for g in range(shards // per):
        block = cs[g * per : (g + 1) * per].reshape(group, lanes)
        for q in range(packs):
            tab[g * group : (g + 1) * group, q * lanes : (q + 1) * lanes] = jnp.dot(
                picks[q], block, preferred_element_type=F32
            ).astype(BF16)

    positives = pos_ref[...]
    positives = jnp.where(core == 0, positives[:, :half_rows], positives[:, half_rows:])
    total = shards * SLOT
    ids = lax.broadcasted_iota(jnp.int32, (total, rows), 0)
    ids = caps * (ids // SLOT) + ids % caps
    piece = (lax.broadcasted_iota(jnp.int32, (total, lanes), 0) % SLOT) // caps

    def score(i):
        each(1, chips, lambda k: chip_copy(k, i, chip_peer(k)).wait_recv())
        projected = xr[0, i].astype(F32)
        for c in range(1, chips):
            projected = projected + xr[c, i].astype(F32)
        scale = lax.rsqrt(jnp.sum(projected * projected, axis=1, keepdims=True) + eps_norm)
        unit = projected * scale
        half = unit.astype(BF16)
        logits = logit_scale * lax.dot_general(
            tab[...], half, (((1,), (1,)), ((), ())), preferred_element_type=F32
        )
        expon = jnp.exp(logits)
        probs = expon * (packs / jnp.sum(expon, axis=0, keepdims=True))
        onehot = (ids == positives[:, i * rows : (i + 1) * rows]).astype(F32)
        dlogits = (probs - onehot).astype(BF16)
        dunit = (logit_scale / packs) * lax.dot_general(
            dlogits, tab[...], (((0,), (0,)), ((), ())), preferred_element_type=F32
        )
        dproj = scale * (dunit - unit * jnp.sum(unit * dunit, axis=1, keepdims=True))
        dp[i, 1] = dproj.astype(BF16)
        dp_copy(i).start()
        term = jnp.zeros((total, lanes), F32)
        for q in range(packs):
            value = jnp.dot(
                dlogits, half[:, q * lanes : (q + 1) * lanes], preferred_element_type=F32
            )
            term = jnp.where(piece == q, value, term)
        dacc[...] = term if i == 0 else dacc[...] + term

    def grad(i):
        dp_copy(i).wait_recv()
        value = lax.dot_general(
            dp[i].reshape(2 * rows, width), wv[...], (((1,), (1,)), ((), ())),
            preferred_element_type=F32,
        ).astype(BF16)
        og[i] = value.reshape(2, rows, depth)
        for which in range(2):
            og_copy(i, which).start()

    sum_copy = pltpu.make_async_remote_copy(
        src_ref=dacc, dst_ref=dpt, send_sem=as_sem, recv_sem=ar_sem,
        device_id=place(mate, t), device_id_type=MESH,
    )

    def give_copy(k, there, here):
        return pltpu.make_async_remote_copy(
            src_ref=dsnd.at[there], dst_ref=drc.at[here],
            send_sem=gs_sem.at[k], recv_sem=gr_sem.at[here],
            device_id=place(sec, shard_peer(k)), device_id_type=MESH,
        )

    for i in range(n_chunks):
        score(i)
        if i == n_chunks - 1:
            sum_copy.start()
        if i >= 1:
            grad(i - 1)
    sum_copy.wait_recv()
    dsnd[...] = (dacc[...] + dpt[...]).astype(BF16).reshape(shards, SLOT, lanes)
    each(1, shards, lambda k: give_copy(k, shard_peer(k), t).start())
    drc[t] = dsnd[t]
    grad(n_chunks - 1)
    each(1, shards, lambda k: give_copy(k, shard_peer(k), shard_peer(k)).wait_recv())
    dcap = logit_scale * jnp.sum(drc[...].astype(F32), axis=0)
    dcap = jnp.concatenate(
        [dcap[q * caps : (q + 1) * caps, :] for q in range(packs)], axis=1
    )
    cg_ref[...] = cap_scale * (
        dcap - cap_unit * jnp.sum(cap_unit * dcap, axis=1, keepdims=True)
    )

    for i in range(n_chunks):
        for which in range(2):
            og_copy(i, which).wait()
        mate_copy(i).wait_send()
        dp_copy(i).wait_send()
        each(1, chips, lambda k: chip_copy(k, i, chip).wait_send())
    sum_copy.wait_send()
    each(1, shards, lambda k: cap_copy(k, t).wait_send())
    each(1, shards, lambda k: give_copy(k, shard_peer(k), t).wait_send())


def write_out(rg_in, cg_in, rg_out, cg_out, sem):
    rows = rg_in.shape[0] // COPIES
    copies = [pltpu.make_async_copy(cg_in, cg_out, sem.at[COPIES])]
    for i in range(COPIES):
        band = pl.ds(i * rows, rows)
        copies.append(pltpu.make_async_copy(rg_in.at[band, :], rg_out.at[band, :], sem.at[i]))
    for copy in copies:
        copy.start()
    for copy in copies:
        copy.wait()


def solution(mesh):
    sections, shards = mesh.shape["section"], mesh.shape["shard"]
    chips = sections // 2

    def on_device(features, proj_weight, captions, positives):
        n_rows, depth = features.shape
        width = proj_weight.shape[1]
        caps = captions.shape[0]
        lanes = width * caps // SLOT
        n = CHUNKS
        rows = n_rows // 2 // n
        dma = pltpu.SemaphoreType.DMA
        any_space = pl.BlockSpec(memory_space=pl.ANY)
        vmem = pl.BlockSpec(memory_space=pltpu.VMEM)
        flops = 4 * n_rows * depth * width
        shapes = (
            jax.ShapeDtypeStruct((n_rows, depth), BF16),
            jax.ShapeDtypeStruct((caps, width), F32),
        )
        grads = pl.pallas_call(
            functools.partial(kernel, sections, shards),
            out_shape=shapes,
            in_specs=[any_space, any_space, vmem, vmem],
            out_specs=(any_space, vmem),
            scratch_shapes=[
                pltpu.VMEM((n, 2, rows, depth), BF16),
                pltpu.VMEM((depth, width), BF16),
                pltpu.VMEM((n, rows, width), F32),
                pltpu.VMEM((n, rows, width), BF16),
                pltpu.VMEM((n, rows, width), BF16),
                pltpu.VMEM((chips, n, rows, width), BF16),
                pltpu.VMEM((n, 2, rows, width), BF16),
                pltpu.VMEM((n, 2, rows, depth), BF16),
                pltpu.VMEM((shards, SLOT, lanes), BF16),
                pltpu.VMEM((shards * SLOT, width), BF16),
                pltpu.VMEM((shards * SLOT, lanes), F32),
                pltpu.VMEM((shards * SLOT, lanes), F32),
                pltpu.VMEM((shards, SLOT, lanes), BF16),
                pltpu.VMEM((shards, SLOT, lanes), BF16),
                dma((n, 2)), dma((PIECES,)), dma((n, 2)),
                dma((n,)), dma((n,)),
                dma((chips, n)), dma((chips, n)),
                dma((n,)), dma((n,)),
                dma((shards,)), dma((shards,)),
                dma, dma,
                dma((shards,)), dma((shards,)),
            ],
            cost_estimate=pl.CostEstimate(
                flops=flops,
                bytes_accessed=2 * (2 * n_rows * depth + depth * width),
                transcendentals=0,
            ),
            compiler_params=pltpu.CompilerParams(
                collective_id=0, has_side_effects=True, vmem_limit_bytes=56 * 1024 * 1024
            ),
        )(features, proj_weight, captions, positives.reshape(1, n_rows))
        return pl.pallas_call(
            write_out,
            out_shape=shapes,
            in_specs=[any_space, any_space],
            out_specs=(any_space, any_space),
            scratch_shapes=[dma((COPIES + 1,))],
            cost_estimate=pl.CostEstimate(
                flops=0, bytes_accessed=4 * n_rows * depth, transcendentals=0
            ),
        )(*grads)

    return jax.shard_map(
        on_device,
        mesh=mesh,
        in_specs=(P("shard", "section"), P("section", None), P("shard", None), P("shard")),
        out_specs=(P("shard", "section"), P("shard", None)),
        check_vma=False,
    )
```

```python
import functools

import jax
import jax.numpy as jnp
from jax import lax
from jax.experimental import pallas as pl
from jax.experimental.pallas import tpu as pltpu
from jax.sharding import PartitionSpec as P

logit_scale = 14.0
eps_norm = 1e-06
MESH = pl.DeviceIdType.MESH
F32 = jnp.float32
BF16 = jnp.bfloat16
SLOT = 16
CHUNKS = 2
COPIES = 4
PIECES = 3


def each(low, high, body):
    if high - low <= 8:
        for k in range(low, high):
            body(k)
    else:
        lax.fori_loop(low, high, lambda k, c: (body(k), c)[1], 0)


def kernel(
    sections, shards, f_hbm, w_hbm, cap_ref, pos_ref, rg_hbm, cg_ref,
    fv, wv, own, psnd, prcv, xs, xr, dp, og, cs, tab, dacc, dpt, dsnd, drc, fin,
    f_sem, w_sem, og_sem, ps_sem, pr_sem, xs_sem, xr_sem, ms_sem, mr_sem, ds_sem, dr_sem,
    cs_sem, cr_sem, as_sem, ar_sem, gs_sem, gr_sem, es_sem, er_sem,
):
    chips = sections // 2
    n_chunks, _, _, rows, width = dp.shape
    depth = wv.shape[0]
    half = chips * rows
    both = 2 * half
    caps = cap_ref.shape[0]
    packs = SLOT // caps
    lanes = width // packs
    sec = lax.axis_index("section")
    t = lax.axis_index("shard")
    core = lax.rem(sec, 2)
    chip = sec // 2
    mate = chip * 2 + (1 - core)

    def chip_peer(k):
        return lax.rem(chip + k, chips)

    def shard_peer(k):
        return lax.rem(t + k, shards)

    def place(c, s):
        return {"section": c, "shard": s}

    def to_mate(src, dst, send, recv):
        return pltpu.make_async_remote_copy(
            src_ref=src, dst_ref=dst, send_sem=send, recv_sem=recv,
            device_id=place(mate, t), device_id_type=MESH,
        )

    def to_chip(k, src, dst, send, recv):
        return pltpu.make_async_remote_copy(
            src_ref=src, dst_ref=dst, send_sem=send, recv_sem=recv,
            device_id=place(chip_peer(k) * 2 + core, t), device_id_type=MESH,
        )

    def to_shard(k, src, dst, send, recv):
        return pltpu.make_async_remote_copy(
            src_ref=src, dst_ref=dst, send_sem=send, recv_sem=recv,
            device_id=place(sec, shard_peer(k)), device_id_type=MESH,
        )

    step = depth // PIECES

    def f_copy(i, which):
        owner = core if which == 1 else 1 - core
        start = pl.multiple_of(i * both + owner * half, half)
        return pltpu.make_async_copy(
            f_hbm.at[pl.ds(start, half), :], fv.at[i, which], f_sem.at[i, which]
        )

    def w_copy(p):
        band = pl.ds(p * step, step)
        return pltpu.make_async_copy(w_hbm.at[band, :], wv.at[band, :], w_sem.at[p])

    def og_copy(i):
        return pltpu.make_async_copy(
            og.at[i], rg_hbm.at[pl.ds(i * both, both), :], og_sem.at[i]
        )

    for which in range(2):
        f_copy(0, which).start()
    for p in range(PIECES):
        w_copy(p).start()
    for i in range(1, n_chunks):
        for which in range(2):
            f_copy(i, which).start()

    barrier = pltpu.get_barrier_semaphore()

    def greet(c, s):
        pl.semaphore_signal(barrier, inc=1, device_id=place(c, s), device_id_type=MESH)

    greet(mate, t)
    each(1, chips, lambda k: greet(chip_peer(k) * 2 + core, t))
    each(1, shards, lambda k: greet(sec, shard_peer(k)))

    cap_float = cap_ref[...].astype(F32)
    cap_scale = lax.rsqrt(jnp.sum(cap_float * cap_float, axis=1, keepdims=True) + eps_norm)
    cap_unit = cap_float * cap_scale
    packed = jnp.concatenate(
        [cap_unit[:, q * lanes : (q + 1) * lanes] for q in range(packs)], axis=0
    )
    cs[t] = packed.astype(BF16)

    def cap_copy(k, source):
        return to_shard(k, cs.at[source], cs.at[source], cs_sem.at[k], cr_sem.at[source])

    def mate_copy(i):
        return to_mate(psnd.at[i], prcv.at[i], ps_sem.at[i], pr_sem.at[i])

    def part_copy(k, i, there, here):
        return to_chip(k, xs.at[i, there], xr.at[here, i], xs_sem.at[k, i], xr_sem.at[here, i])

    def chip_sum(i):
        mate_copy(i).wait_recv()
        value = own[i] + prcv[i].astype(F32)
        own[i] = value
        xs[i] = value.astype(BF16).reshape(chips, rows, width)
        each(1, chips, lambda k: part_copy(k, i, chip_peer(k), chip).start())

    for i in range(n_chunks):
        for which in range(2):
            f_copy(i, which).wait()
        if i == 0:
            part = None
            for p in range(PIECES):
                w_copy(p).wait()
                band = slice(p * step, (p + 1) * step)
                term = jnp.dot(
                    fv[i, :, :, band].reshape(both, step), wv[band, :],
                    preferred_element_type=F32,
                )
                part = term if part is None else part + term
        else:
            part = jnp.dot(fv[i].reshape(both, depth), wv[...], preferred_element_type=F32)
        psnd[i] = part[:half].astype(BF16)
        own[i] = part[half:]
        if i == 0:
            pl.semaphore_wait(barrier, 1 + (chips - 1) + (shards - 1))
        mate_copy(i).start()
        if i == 0:
            each(1, shards, lambda k: cap_copy(k, t).start())
        if i >= 1:
            chip_sum(i - 1)
    chip_sum(n_chunks - 1)

    each(1, shards, lambda k: cap_copy(k, shard_peer(k)).wait_recv())
    per = min(8, shards)
    group = per * SLOT
    ra = lax.broadcasted_iota(jnp.int32, (group, group), 0)
    rb = lax.broadcasted_iota(jnp.int32, (group, group), 1)
    same = jnp.logical_and(ra // SLOT == rb // SLOT, ra % caps == rb % caps)
    picks = [
        jnp.logical_and(same, (rb % SLOT) // caps == q).astype(F32).astype(BF16)
        for q in range(packs)
    ]
    for g in range(shards // per):
        block = cs[g * per : (g + 1) * per].reshape(group, lanes)
        for q in range(packs):
            tab[g * group : (g + 1) * group, q * lanes : (q + 1) * lanes] = jnp.dot(
                picks[q], block, preferred_element_type=F32
            ).astype(BF16)

    positives = pos_ref[...]
    mine = core * chips + chip
    total = shards * SLOT
    ids = lax.broadcasted_iota(jnp.int32, (total, rows), 0)
    ids = caps * (ids // SLOT) + ids % caps
    piece = (lax.broadcasted_iota(jnp.int32, (total, lanes), 0) % SLOT) // caps

    def dp_chip(k, i, source):
        block = dp.at[i, core, source]
        return to_chip(k, block, block, ds_sem.at[k, i], dr_sem.at[source, i])

    def dp_mate(i, source, side):
        block = dp.at[i, side, source]
        return to_mate(block, block, ms_sem.at[source, i], mr_sem.at[source, i])

    def score(i):
        each(1, chips, lambda k: part_copy(k, i, chip_peer(k), chip_peer(k)).wait_recv())
        start = pl.multiple_of(chip * rows, rows)
        projected = own[i, pl.ds(start, rows), :]
        for k in range(1, chips):
            projected = projected + xr[chip_peer(k), i].astype(F32)
        scale = lax.rsqrt(jnp.sum(projected * projected, axis=1, keepdims=True) + eps_norm)
        unit = projected * scale
        unit_half = unit.astype(BF16)
        logits = logit_scale * lax.dot_general(
            tab[...], unit_half, (((1,), (1,)), ((), ())), preferred_element_type=F32
        )
        expon = jnp.exp(logits)
        probs = expon * (packs / jnp.sum(expon, axis=0, keepdims=True))
        index = positives[:, i * both : i * both + rows]
        for j in range(1, sections):
            low = i * both + j * rows
            index = jnp.where(mine == j, positives[:, low : low + rows], index)
        onehot = (ids == index).astype(F32)
        dlogits = (probs - onehot).astype(BF16)
        dunit = (logit_scale / packs) * lax.dot_general(
            dlogits, tab[...], (((0,), (0,)), ((), ())), preferred_element_type=F32
        )
        dproj = scale * (dunit - unit * jnp.sum(unit * dunit, axis=1, keepdims=True))
        dp[i, core, chip] = dproj.astype(BF16)
        each(1, chips, lambda k: dp_chip(k, i, chip).start())
        dp_mate(i, chip, core).start()
        term = jnp.zeros((total, lanes), F32)
        for q in range(packs):
            value = jnp.dot(
                dlogits, unit_half[:, q * lanes : (q + 1) * lanes], preferred_element_type=F32
            )
            term = jnp.where(piece == q, value, term)
        dacc[...] = term if i == 0 else dacc[...] + term

    def forward(i):
        def one(k):
            dp_chip(k, i, chip_peer(k)).wait_recv()
            dp_mate(i, chip_peer(k), core).start()

        each(1, chips, one)

    def grad(i):
        each(0, chips, lambda c: dp_mate(i, c, 1 - core).wait_recv())
        og[i] = lax.dot_general(
            dp[i].reshape(both, width), wv[...], (((1,), (1,)), ((), ())),
            preferred_element_type=F32,
        ).astype(BF16)
        og_copy(i).start()

    sum_copy = to_mate(dacc, dpt, as_sem, ar_sem)

    def give_copy(k, there, here):
        return to_shard(k, dsnd.at[there], drc.at[here], gs_sem.at[k], gr_sem.at[here])

    def end_copy(k, source):
        return to_chip(k, fin.at[source], fin.at[source], es_sem.at[k], er_sem.at[source])

    for i in range(n_chunks):
        score(i)
    sum_copy.start()
    forward(0)
    sum_copy.wait_recv()
    dsnd[...] = (dacc[...] + dpt[...]).astype(BF16).reshape(shards, SLOT, lanes)
    each(1, shards, lambda k: give_copy(k, shard_peer(k), t).start())
    drc[t] = dsnd[t]
    for i in range(n_chunks):
        grad(i)
        if i < n_chunks - 1:
            forward(i + 1)
    each(1, shards, lambda k: give_copy(k, shard_peer(k), shard_peer(k)).wait_recv())
    fin[chip] = jnp.sum(drc[...].astype(F32), axis=0)
    each(1, chips, lambda k: end_copy(k, chip).start())
    each(1, chips, lambda k: end_copy(k, chip_peer(k)).wait_recv())
    dcap = logit_scale * jnp.sum(fin[...], axis=0)
    dcap = jnp.concatenate(
        [dcap[q * caps : (q + 1) * caps, :] for q in range(packs)], axis=1
    )
    cg_ref[...] = cap_scale * (
        dcap - cap_unit * jnp.sum(cap_unit * dcap, axis=1, keepdims=True)
    )

    for i in range(n_chunks):
        og_copy(i).wait()
        mate_copy(i).wait_send()
        each(1, chips, lambda k: part_copy(k, i, chip_peer(k), chip).wait_send())
        each(1, chips, lambda k: dp_chip(k, i, chip).wait_send())
        each(0, chips, lambda c: dp_mate(i, c, core).wait_send())
    sum_copy.wait_send()
    each(1, shards, lambda k: cap_copy(k, t).wait_send())
    each(1, shards, lambda k: give_copy(k, shard_peer(k), t).wait_send())
    each(1, chips, lambda k: end_copy(k, chip).wait_send())


def write_out(rg_in, cg_in, rg_out, cg_out, rg_buf, cg_buf, in_sem, out_sem):
    rows = rg_in.shape[0] // COPIES
    moves = []
    for i in range(COPIES):
        band = pl.ds(i * rows, rows)
        moves.append((rg_in.at[band, :], rg_buf.at[band, :], rg_out.at[band, :]))
    moves.append((cg_in, cg_buf, cg_out))
    loads = [pltpu.make_async_copy(a, b, in_sem.at[j]) for j, (a, b, c) in enumerate(moves)]
    stores = [pltpu.make_async_copy(b, c, out_sem.at[j]) for j, (a, b, c) in enumerate(moves)]
    for load in loads:
        load.start()
    for load, store in zip(loads, stores):
        load.wait()
        store.start()
    for store in stores:
        store.wait()


def solution(mesh):
    sections, shards = mesh.shape["section"], mesh.shape["shard"]
    chips = sections // 2

    def on_device(features, proj_weight, captions, positives):
        n_rows, depth = features.shape
        width = proj_weight.shape[1]
        caps = captions.shape[0]
        lanes = width * caps // SLOT
        n = CHUNKS
        rows = n_rows // sections // n
        half = chips * rows
        dma = pltpu.SemaphoreType.DMA
        any_space = pl.BlockSpec(memory_space=pl.ANY)
        vmem = pl.BlockSpec(memory_space=pltpu.VMEM)
        flops = 4 * n_rows * depth * width
        shapes = (
            jax.ShapeDtypeStruct((n_rows, depth), BF16),
            jax.ShapeDtypeStruct((caps, width), F32),
        )
        grads = pl.pallas_call(
            functools.partial(kernel, sections, shards),
            out_shape=shapes,
            in_specs=[any_space, any_space, vmem, vmem],
            out_specs=(any_space, vmem),
            scratch_shapes=[
                pltpu.VMEM((n, 2, half, depth), BF16),
                pltpu.VMEM((depth, width), BF16),
                pltpu.VMEM((n, half, width), F32),
                pltpu.VMEM((n, half, width), BF16),
                pltpu.VMEM((n, half, width), BF16),
                pltpu.VMEM((n, chips, rows, width), BF16),
                pltpu.VMEM((chips, n, rows, width), BF16),
                pltpu.VMEM((n, 2, chips, rows, width), BF16),
                pltpu.VMEM((n, 2 * half, depth), BF16),
                pltpu.VMEM((shards, SLOT, lanes), BF16),
                pltpu.VMEM((shards * SLOT, width), BF16),
                pltpu.VMEM((shards * SLOT, lanes), F32),
                pltpu.VMEM((shards * SLOT, lanes), F32),
                pltpu.VMEM((shards, SLOT, lanes), BF16),
                pltpu.VMEM((shards, SLOT, lanes), BF16),
                pltpu.VMEM((chips, SLOT, lanes), F32),
                dma((n, 2)), dma((PIECES,)), dma((n,)),
                dma((n,)), dma((n,)),
                dma((chips, n)), dma((chips, n)),
                dma((chips, n)), dma((chips, n)),
                dma((chips, n)), dma((chips, n)),
                dma((shards,)), dma((shards,)),
                dma, dma,
                dma((shards,)), dma((shards,)),
                dma((chips,)), dma((chips,)),
            ],
            cost_estimate=pl.CostEstimate(
                flops=flops,
                bytes_accessed=2 * (2 * n_rows * depth + depth * width),
                transcendentals=0,
            ),
            compiler_params=pltpu.CompilerParams(
                collective_id=0, has_side_effects=True, vmem_limit_bytes=56 * 1024 * 1024
            ),
        )(features, proj_weight, captions, positives.reshape(1, n_rows))
        return pl.pallas_call(
            write_out,
            out_shape=shapes,
            in_specs=[any_space, any_space],
            out_specs=(any_space, any_space),
            scratch_shapes=[
                pltpu.VMEM((n_rows, depth), BF16),
                pltpu.VMEM((caps, width), F32),
                dma((COPIES + 1,)), dma((COPIES + 1,)),
            ],
            cost_estimate=pl.CostEstimate(
                flops=0, bytes_accessed=4 * n_rows * depth, transcendentals=0
            ),
        )(*grads)

    return jax.shard_map(
        on_device,
        mesh=mesh,
        in_specs=(P("shard", "section"), P("section", None), P("shard", None), P("shard")),
        out_specs=(P("shard", "section"), P("shard", None)),
        check_vma=False,
    )
```

```python
import functools

import jax
import jax.numpy as jnp
from jax import lax
from jax.experimental import pallas as pl
from jax.experimental.pallas import tpu as pltpu
from jax.sharding import PartitionSpec as P

logit_scale = 14.0
eps_norm = 1e-06
MESH = pl.DeviceIdType.MESH
F32 = jnp.float32
BF16 = jnp.bfloat16
SLOT = 16
CHUNKS = 2
COPIES = 4
PIECES = 3


def each(low, high, body):
    if high - low <= 8:
        for k in range(low, high):
            body(k)
    else:
        lax.fori_loop(low, high, lambda k, c: (body(k), c)[1], 0)


def kernel(
    sections, shards, f_hbm, w_hbm, cap_ref, pos_ref, rg_ref, cg_ref,
    fv, wv, own, psnd, prcv, xs, xr, dp, cs, tab, dacc, dpt, dsnd, drc, fin,
    f_sem, w_sem, ps_sem, pr_sem, xs_sem, xr_sem, ms_sem, mr_sem, ds_sem, dr_sem,
    cs_sem, cr_sem, as_sem, ar_sem, gs_sem, gr_sem, es_sem, er_sem,
):
    chips = sections // 2
    n_chunks, _, _, rows, width = dp.shape
    depth = wv.shape[0]
    half = chips * rows
    both = 2 * half
    caps = cap_ref.shape[0]
    packs = SLOT // caps
    lanes = width // packs
    sec = lax.axis_index("section")
    t = lax.axis_index("shard")
    core = lax.rem(sec, 2)
    chip = sec // 2
    mate = chip * 2 + (1 - core)

    def chip_peer(k):
        return lax.rem(chip + k, chips)

    def shard_peer(k):
        return lax.rem(t + k, shards)

    def place(c, s):
        return {"section": c, "shard": s}

    def to_mate(src, dst, send, recv):
        return pltpu.make_async_remote_copy(
            src_ref=src, dst_ref=dst, send_sem=send, recv_sem=recv,
            device_id=place(mate, t), device_id_type=MESH,
        )

    def to_chip(k, src, dst, send, recv):
        return pltpu.make_async_remote_copy(
            src_ref=src, dst_ref=dst, send_sem=send, recv_sem=recv,
            device_id=place(chip_peer(k) * 2 + core, t), device_id_type=MESH,
        )

    def to_shard(k, src, dst, send, recv):
        return pltpu.make_async_remote_copy(
            src_ref=src, dst_ref=dst, send_sem=send, recv_sem=recv,
            device_id=place(sec, shard_peer(k)), device_id_type=MESH,
        )

    step = depth // PIECES

    def f_copy(i, which):
        owner = core if which == 1 else 1 - core
        start = pl.multiple_of(i * both + owner * half, half)
        return pltpu.make_async_copy(
            f_hbm.at[pl.ds(start, half), :], fv.at[i, which], f_sem.at[i, which]
        )

    def w_copy(p):
        band = pl.ds(p * step, step)
        return pltpu.make_async_copy(w_hbm.at[band, :], wv.at[band, :], w_sem.at[p])

    for which in range(2):
        f_copy(0, which).start()
    for p in range(PIECES):
        w_copy(p).start()
    for i in range(1, n_chunks):
        for which in range(2):
            f_copy(i, which).start()

    barrier = pltpu.get_barrier_semaphore()

    def greet(c, s):
        pl.semaphore_signal(barrier, inc=1, device_id=place(c, s), device_id_type=MESH)

    greet(mate, t)
    each(1, chips, lambda k: greet(chip_peer(k) * 2 + core, t))
    each(1, shards, lambda k: greet(sec, shard_peer(k)))

    cap_float = cap_ref[...].astype(F32)
    cap_scale = lax.rsqrt(jnp.sum(cap_float * cap_float, axis=1, keepdims=True) + eps_norm)
    cap_unit = cap_float * cap_scale
    packed = jnp.concatenate(
        [cap_unit[:, q * lanes : (q + 1) * lanes] for q in range(packs)], axis=0
    )
    cs[t] = packed.astype(BF16)

    def cap_copy(k, source):
        return to_shard(k, cs.at[source], cs.at[source], cs_sem.at[k], cr_sem.at[source])

    def mate_copy(i):
        return to_mate(psnd.at[i], prcv.at[i], ps_sem.at[i], pr_sem.at[i])

    def part_copy(k, i, there, here):
        return to_chip(k, xs.at[i, there], xr.at[here, i], xs_sem.at[k, i], xr_sem.at[here, i])

    def chip_sum(i):
        mate_copy(i).wait_recv()
        value = own[i] + prcv[i].astype(F32)
        own[i] = value
        xs[i] = value.astype(BF16).reshape(chips, rows, width)
        each(1, chips, lambda k: part_copy(k, i, chip_peer(k), chip).start())

    for i in range(n_chunks):
        for which in range(2):
            f_copy(i, which).wait()
        part = None
        for p in range(PIECES):
            if i == 0:
                w_copy(p).wait()
            band = slice(p * step, (p + 1) * step)
            term = jnp.dot(
                fv[i, :, :, band].reshape(both, step), wv[band, :], preferred_element_type=F32
            )
            part = term if part is None else part + term
            if i >= 1 and p == PIECES - 2:
                chip_sum(i - 1)
        psnd[i] = part[:half].astype(BF16)
        own[i] = part[half:]
        if i == 0:
            pl.semaphore_wait(barrier, 1 + (chips - 1) + (shards - 1))
        mate_copy(i).start()
        if i == 0:
            each(1, shards, lambda k: cap_copy(k, t).start())
    chip_sum(n_chunks - 1)

    each(1, shards, lambda k: cap_copy(k, shard_peer(k)).wait_recv())
    per = min(8, shards)
    group = per * SLOT
    ra = lax.broadcasted_iota(jnp.int32, (group, group), 0)
    rb = lax.broadcasted_iota(jnp.int32, (group, group), 1)
    same = jnp.logical_and(ra // SLOT == rb // SLOT, ra % caps == rb % caps)
    picks = [
        jnp.logical_and(same, (rb % SLOT) // caps == q).astype(F32).astype(BF16)
        for q in range(packs)
    ]
    for g in range(shards // per):
        block = cs[g * per : (g + 1) * per].reshape(group, lanes)
        for q in range(packs):
            tab[g * group : (g + 1) * group, q * lanes : (q + 1) * lanes] = jnp.dot(
                picks[q], block, preferred_element_type=F32
            ).astype(BF16)

    positives = pos_ref[...]
    mine = core * chips + chip
    total = shards * SLOT
    ids = lax.broadcasted_iota(jnp.int32, (total, rows), 0)
    ids = caps * (ids // SLOT) + ids % caps
    piece = (lax.broadcasted_iota(jnp.int32, (total, lanes), 0) % SLOT) // caps

    def dp_chip(k, i, source):
        block = dp.at[i, core, source]
        return to_chip(k, block, block, ds_sem.at[k, i], dr_sem.at[source, i])

    def dp_mate(i, source, side):
        block = dp.at[i, side, source]
        return to_mate(block, block, ms_sem.at[source, i], mr_sem.at[source, i])

    def score(i):
        each(1, chips, lambda k: part_copy(k, i, chip_peer(k), chip_peer(k)).wait_recv())
        start = pl.multiple_of(chip * rows, rows)
        projected = own[i, pl.ds(start, rows), :]
        for k in range(1, chips):
            projected = projected + xr[chip_peer(k), i].astype(F32)
        scale = lax.rsqrt(jnp.sum(projected * projected, axis=1, keepdims=True) + eps_norm)
        unit = projected * scale
        unit_half = unit.astype(BF16)
        logits = logit_scale * lax.dot_general(
            tab[...], unit_half, (((1,), (1,)), ((), ())), preferred_element_type=F32
        )
        expon = jnp.exp(logits)
        probs = expon * (packs / jnp.sum(expon, axis=0, keepdims=True))
        index = positives[:, i * both : i * both + rows]
        for j in range(1, sections):
            low = i * both + j * rows
            index = jnp.where(mine == j, positives[:, low : low + rows], index)
        onehot = (ids == index).astype(F32)
        dlogits = (probs - onehot).astype(BF16)
        dunit = (logit_scale / packs) * lax.dot_general(
            dlogits, tab[...], (((0,), (0,)), ((), ())), preferred_element_type=F32
        )
        dproj = scale * (dunit - unit * jnp.sum(unit * dunit, axis=1, keepdims=True))
        dp[i, core, chip] = dproj.astype(BF16)
        each(1, chips, lambda k: dp_chip(k, i, chip).start())
        dp_mate(i, chip, core).start()
        term = jnp.zeros((total, lanes), F32)
        for q in range(packs):
            value = jnp.dot(
                dlogits, unit_half[:, q * lanes : (q + 1) * lanes], preferred_element_type=F32
            )
            term = jnp.where(piece == q, value, term)
        dacc[...] = term if i == 0 else dacc[...] + term

    def forward(i):
        def one(k):
            dp_chip(k, i, chip_peer(k)).wait_recv()
            dp_mate(i, chip_peer(k), core).start()

        each(1, chips, one)

    def grad(i, part, parts):
        if part == 0:
            each(0, chips, lambda c: dp_mate(i, c, 1 - core).wait_recv())
        size = depth // parts
        band = slice(part * size, (part + 1) * size)
        rg_ref[i * both : (i + 1) * both, band] = lax.dot_general(
            dp[i].reshape(both, width), wv[band, :], (((1,), (1,)), ((), ())),
            preferred_element_type=F32,
        ).astype(BF16)

    sum_copy = to_mate(dacc, dpt, as_sem, ar_sem)

    def give_copy(k, there, here):
        return to_shard(k, dsnd.at[there], drc.at[here], gs_sem.at[k], gr_sem.at[here])

    def end_copy(k, source):
        return to_chip(k, fin.at[source], fin.at[source], es_sem.at[k], er_sem.at[source])

    for i in range(n_chunks):
        score(i)
    sum_copy.start()
    forward(0)
    sum_copy.wait_recv()
    dsnd[...] = (dacc[...] + dpt[...]).astype(BF16).reshape(shards, SLOT, lanes)
    each(1, shards, lambda k: give_copy(k, shard_peer(k), t).start())
    drc[t] = dsnd[t]
    for i in range(n_chunks - 1):
        grad(i, 0, 1)
        forward(i + 1)
    grad(n_chunks - 1, 0, 2)
    each(1, shards, lambda k: give_copy(k, shard_peer(k), shard_peer(k)).wait_recv())
    fin[chip] = jnp.sum(drc[...].astype(F32), axis=0)
    each(1, chips, lambda k: end_copy(k, chip).start())
    grad(n_chunks - 1, 1, 2)
    each(1, chips, lambda k: end_copy(k, chip_peer(k)).wait_recv())
    dcap = logit_scale * jnp.sum(fin[...], axis=0)
    dcap = jnp.concatenate(
        [dcap[q * caps : (q + 1) * caps, :] for q in range(packs)], axis=1
    )
    cg_ref[...] = cap_scale * (
        dcap - cap_unit * jnp.sum(cap_unit * dcap, axis=1, keepdims=True)
    )

    for i in range(n_chunks):
        mate_copy(i).wait_send()
        each(1, chips, lambda k: part_copy(k, i, chip_peer(k), chip).wait_send())
        each(1, chips, lambda k: dp_chip(k, i, chip).wait_send())
        each(0, chips, lambda c: dp_mate(i, c, core).wait_send())
    sum_copy.wait_send()
    each(1, shards, lambda k: cap_copy(k, t).wait_send())
    each(1, shards, lambda k: give_copy(k, shard_peer(k), t).wait_send())
    each(1, chips, lambda k: end_copy(k, chip).wait_send())


def write_out(rg_in, cg_in, rg_out, cg_out, sem):
    rows = rg_in.shape[0] // COPIES
    copies = [pltpu.make_async_copy(cg_in, cg_out, sem.at[COPIES])]
    for i in range(COPIES):
        band = pl.ds(i * rows, rows)
        copies.append(pltpu.make_async_copy(rg_in.at[band, :], rg_out.at[band, :], sem.at[i]))
    for copy in copies:
        copy.start()
    for copy in copies:
        copy.wait()


def solution(mesh):
    sections, shards = mesh.shape["section"], mesh.shape["shard"]
    chips = sections // 2

    def on_device(features, proj_weight, captions, positives):
        n_rows, depth = features.shape
        width = proj_weight.shape[1]
        caps = captions.shape[0]
        lanes = width * caps // SLOT
        n = CHUNKS
        rows = n_rows // sections // n
        half = chips * rows
        dma = pltpu.SemaphoreType.DMA
        any_space = pl.BlockSpec(memory_space=pl.ANY)
        vmem = pl.BlockSpec(memory_space=pltpu.VMEM)
        flops = 4 * n_rows * depth * width
        shapes = (
            jax.ShapeDtypeStruct((n_rows, depth), BF16),
            jax.ShapeDtypeStruct((caps, width), F32),
        )
        grads = pl.pallas_call(
            functools.partial(kernel, sections, shards),
            out_shape=(
                pltpu.VMEM((n_rows, depth), BF16), pltpu.VMEM((caps, width), F32)
            ),
            in_specs=[any_space, any_space, vmem, vmem],
            out_specs=(vmem, vmem),
            scratch_shapes=[
                pltpu.VMEM((n, 2, half, depth), BF16),
                pltpu.VMEM((depth, width), BF16),
                pltpu.VMEM((n, half, width), F32),
                pltpu.VMEM((n, half, width), BF16),
                pltpu.VMEM((n, half, width), BF16),
                pltpu.VMEM((n, chips, rows, width), BF16),
                pltpu.VMEM((chips, n, rows, width), BF16),
                pltpu.VMEM((n, 2, chips, rows, width), BF16),
                pltpu.VMEM((shards, SLOT, lanes), BF16),
                pltpu.VMEM((shards * SLOT, width), BF16),
                pltpu.VMEM((shards * SLOT, lanes), F32),
                pltpu.VMEM((shards * SLOT, lanes), F32),
                pltpu.VMEM((shards, SLOT, lanes), BF16),
                pltpu.VMEM((shards, SLOT, lanes), BF16),
                pltpu.VMEM((chips, SLOT, lanes), F32),
                dma((n, 2)), dma((PIECES,)),
                dma((n,)), dma((n,)),
                dma((chips, n)), dma((chips, n)),
                dma((chips, n)), dma((chips, n)),
                dma((chips, n)), dma((chips, n)),
                dma((shards,)), dma((shards,)),
                dma, dma,
                dma((shards,)), dma((shards,)),
                dma((chips,)), dma((chips,)),
            ],
            cost_estimate=pl.CostEstimate(
                flops=flops,
                bytes_accessed=2 * (2 * n_rows * depth + depth * width),
                transcendentals=0,
            ),
            compiler_params=pltpu.CompilerParams(
                collective_id=0, has_side_effects=True, vmem_limit_bytes=56 * 1024 * 1024
            ),
        )(features, proj_weight, captions, positives.reshape(1, n_rows))
        return pl.pallas_call(
            write_out,
            out_shape=shapes,
            in_specs=[vmem, vmem],
            out_specs=(any_space, any_space),
            scratch_shapes=[
                dma((COPIES + 1,)),
            ],
            cost_estimate=pl.CostEstimate(
                flops=0, bytes_accessed=4 * n_rows * depth, transcendentals=0
            ),
        )(*grads)

    return jax.shard_map(
        on_device,
        mesh=mesh,
        in_specs=(P("shard", "section"), P("section", None), P("shard", None), P("shard")),
        out_specs=(P("shard", "section"), P("shard", None)),
        check_vma=False,
    )
```

```python
import functools

import jax
import jax.numpy as jnp
from jax import lax
from jax.experimental import pallas as pl
from jax.experimental.pallas import tpu as pltpu
from jax.sharding import PartitionSpec as P

logit_scale = 14.0
eps_norm = 1e-06
MESH = pl.DeviceIdType.MESH
F32 = jnp.float32
BF16 = jnp.bfloat16
SLOT = 16
CHUNKS = 2
PIECES = 3


def each(low, high, body):
    if high - low <= 8:
        for k in range(low, high):
            body(k)
    else:
        lax.fori_loop(low, high, lambda k, c: (body(k), c)[1], 0)


def kernel(
    sections, shards, f_hbm, w_hbm, cap_ref, pos_ref, rg_ref, cg_ref,
    fv, wv, own, psnd, prcv, xs, xr, dp, cs, tab, dacc, dpt, dsnd, drc, fin,
    f_sem, w_sem, ps_sem, pr_sem, xs_sem, xr_sem, ms_sem, mr_sem, ds_sem, dr_sem,
    cs_sem, cr_sem, as_sem, ar_sem, gs_sem, gr_sem, es_sem, er_sem,
):
    chips = sections // 2
    n_chunks, _, _, rows, width = dp.shape
    depth = wv.shape[0]
    half = chips * rows
    both = 2 * half
    caps = cap_ref.shape[0]
    packs = SLOT // caps
    lanes = width // packs
    sec = lax.axis_index("section")
    t = lax.axis_index("shard")
    core = lax.rem(sec, 2)
    chip = sec // 2
    mate = chip * 2 + (1 - core)

    def chip_peer(k):
        return lax.rem(chip + k, chips)

    def shard_peer(k):
        return lax.rem(t + k, shards)

    def place(c, s):
        return {"section": c, "shard": s}

    def to_mate(src, dst, send, recv):
        return pltpu.make_async_remote_copy(
            src_ref=src, dst_ref=dst, send_sem=send, recv_sem=recv,
            device_id=place(mate, t), device_id_type=MESH,
        )

    def to_chip(k, src, dst, send, recv):
        return pltpu.make_async_remote_copy(
            src_ref=src, dst_ref=dst, send_sem=send, recv_sem=recv,
            device_id=place(chip_peer(k) * 2 + core, t), device_id_type=MESH,
        )

    def to_shard(k, src, dst, send, recv):
        return pltpu.make_async_remote_copy(
            src_ref=src, dst_ref=dst, send_sem=send, recv_sem=recv,
            device_id=place(sec, shard_peer(k)), device_id_type=MESH,
        )

    step = depth // PIECES

    def f_copy(i, which):
        owner = core if which == 1 else 1 - core
        start = pl.multiple_of(i * both + owner * half, half)
        return pltpu.make_async_copy(
            f_hbm.at[pl.ds(start, half), :], fv.at[i, which], f_sem.at[i, which]
        )

    def w_copy(p):
        band = pl.ds(p * step, step)
        return pltpu.make_async_copy(w_hbm.at[band, :], wv.at[band, :], w_sem.at[p])

    for which in range(2):
        f_copy(0, which).start()
    for p in range(PIECES):
        w_copy(p).start()
    for i in range(1, n_chunks):
        for which in range(2):
            f_copy(i, which).start()

    barrier = pltpu.get_barrier_semaphore()

    def greet(c, s):
        pl.semaphore_signal(barrier, inc=1, device_id=place(c, s), device_id_type=MESH)

    greet(mate, t)
    each(1, chips, lambda k: greet(chip_peer(k) * 2 + core, t))
    each(1, shards, lambda k: greet(sec, shard_peer(k)))

    cap_float = cap_ref[...].astype(F32)
    cap_scale = lax.rsqrt(jnp.sum(cap_float * cap_float, axis=1, keepdims=True) + eps_norm)
    cap_unit = cap_float * cap_scale
    packed = jnp.concatenate(
        [cap_unit[:, q * lanes : (q + 1) * lanes] for q in range(packs)], axis=0
    )
    cs[t] = packed.astype(BF16)

    def cap_copy(k, source):
        return to_shard(k, cs.at[source], cs.at[source], cs_sem.at[k], cr_sem.at[source])

    def mate_copy(i):
        return to_mate(psnd.at[i], prcv.at[i], ps_sem.at[i], pr_sem.at[i])

    def part_copy(k, i, there, here):
        return to_chip(k, xs.at[i, there], xr.at[here, i], xs_sem.at[k, i], xr_sem.at[here, i])

    def chip_sum(i):
        mate_copy(i).wait_recv()
        value = own[i] + prcv[i].astype(F32)
        own[i] = value
        xs[i] = value.astype(BF16).reshape(chips, rows, width)
        each(1, chips, lambda k: part_copy(k, i, chip_peer(k), chip).start())

    for i in range(n_chunks):
        for which in range(2):
            f_copy(i, which).wait()
        part = None
        for p in range(PIECES):
            if i == 0:
                w_copy(p).wait()
            band = slice(p * step, (p + 1) * step)
            term = jnp.dot(
                fv[i, :, :, band].reshape(both, step), wv[band, :], preferred_element_type=F32
            )
            part = term if part is None else part + term
            if i >= 1 and p == PIECES - 2:
                chip_sum(i - 1)
        psnd[i] = part[:half].astype(BF16)
        own[i] = part[half:]
        if i == 0:
            pl.semaphore_wait(barrier, 1 + (chips - 1) + (shards - 1))
        mate_copy(i).start()
        if i == 0:
            each(1, shards, lambda k: cap_copy(k, t).start())
    chip_sum(n_chunks - 1)

    each(1, shards, lambda k: cap_copy(k, shard_peer(k)).wait_recv())
    per = min(8, shards)
    group = per * SLOT
    ra = lax.broadcasted_iota(jnp.int32, (group, group), 0)
    rb = lax.broadcasted_iota(jnp.int32, (group, group), 1)
    same = jnp.logical_and(ra // SLOT == rb // SLOT, ra % caps == rb % caps)
    picks = [
        jnp.logical_and(same, (rb % SLOT) // caps == q).astype(F32).astype(BF16)
        for q in range(packs)
    ]
    for g in range(shards // per):
        block = cs[g * per : (g + 1) * per].reshape(group, lanes)
        for q in range(packs):
            tab[g * group : (g + 1) * group, q * lanes : (q + 1) * lanes] = jnp.dot(
                picks[q], block, preferred_element_type=F32
            ).astype(BF16)

    positives = pos_ref[...]
    mine = core * chips + chip
    total = shards * SLOT
    ids = lax.broadcasted_iota(jnp.int32, (total, rows), 0)
    ids = caps * (ids // SLOT) + ids % caps
    piece = (lax.broadcasted_iota(jnp.int32, (total, lanes), 0) % SLOT) // caps

    def dp_chip(k, i, source):
        block = dp.at[i, core, source]
        return to_chip(k, block, block, ds_sem.at[k, i], dr_sem.at[source, i])

    def dp_mate(i, source, side):
        block = dp.at[i, side, source]
        return to_mate(block, block, ms_sem.at[source, i], mr_sem.at[source, i])

    def score(i):
        each(1, chips, lambda k: part_copy(k, i, chip_peer(k), chip_peer(k)).wait_recv())
        start = pl.multiple_of(chip * rows, rows)
        projected = own[i, pl.ds(start, rows), :]
        for k in range(1, chips):
            projected = projected + xr[chip_peer(k), i].astype(F32)
        scale = lax.rsqrt(jnp.sum(projected * projected, axis=1, keepdims=True) + eps_norm)
        unit = projected * scale
        unit_half = unit.astype(BF16)
        logits = logit_scale * lax.dot_general(
            tab[...], unit_half, (((1,), (1,)), ((), ())), preferred_element_type=F32
        )
        expon = jnp.exp(logits)
        probs = expon * (packs / jnp.sum(expon, axis=0, keepdims=True))
        index = positives[:, i * both : i * both + rows]
        for j in range(1, sections):
            low = i * both + j * rows
            index = jnp.where(mine == j, positives[:, low : low + rows], index)
        onehot = (ids == index).astype(F32)
        dlogits = (probs - onehot).astype(BF16)
        dunit = (logit_scale / packs) * lax.dot_general(
            dlogits, tab[...], (((0,), (0,)), ((), ())), preferred_element_type=F32
        )
        dproj = scale * (dunit - unit * jnp.sum(unit * dunit, axis=1, keepdims=True))
        dp[i, core, chip] = dproj.astype(BF16)
        each(1, chips, lambda k: dp_chip(k, i, chip).start())
        dp_mate(i, chip, core).start()
        term = jnp.zeros((total, lanes), F32)
        for q in range(packs):
            value = jnp.dot(
                dlogits, unit_half[:, q * lanes : (q + 1) * lanes], preferred_element_type=F32
            )
            term = jnp.where(piece == q, value, term)
        dacc[...] = term if i == 0 else dacc[...] + term

    def forward(i):
        def one(k):
            dp_chip(k, i, chip_peer(k)).wait_recv()
            dp_mate(i, chip_peer(k), core).start()

        each(1, chips, one)

    def grad(i, part, parts):
        if part == 0:
            each(0, chips, lambda c: dp_mate(i, c, 1 - core).wait_recv())
        size = depth // parts
        band = slice(part * size, (part + 1) * size)
        rg_ref[i * both : (i + 1) * both, band] = lax.dot_general(
            dp[i].reshape(both, width), wv[band, :], (((1,), (1,)), ((), ())),
            preferred_element_type=F32,
        ).astype(BF16)

    sum_copy = to_mate(dacc, dpt, as_sem, ar_sem)

    def give_copy(k, there, here):
        return to_shard(k, dsnd.at[there], drc.at[here], gs_sem.at[k], gr_sem.at[here])

    def end_copy(k, source):
        return to_chip(k, fin.at[source], fin.at[source], es_sem.at[k], er_sem.at[source])

    for i in range(n_chunks):
        score(i)
    sum_copy.start()
    forward(0)
    sum_copy.wait_recv()
    dsnd[...] = (dacc[...] + dpt[...]).astype(BF16).reshape(shards, SLOT, lanes)
    each(1, shards, lambda k: give_copy(k, shard_peer(k), t).start())
    drc[t] = dsnd[t]
    for i in range(n_chunks - 1):
        grad(i, 0, 1)
        forward(i + 1)
    grad(n_chunks - 1, 0, 2)
    each(1, shards, lambda k: give_copy(k, shard_peer(k), shard_peer(k)).wait_recv())
    fin[chip] = jnp.sum(drc[...].astype(F32), axis=0)
    each(1, chips, lambda k: end_copy(k, chip).start())
    grad(n_chunks - 1, 1, 2)
    each(1, chips, lambda k: end_copy(k, chip_peer(k)).wait_recv())
    dcap = logit_scale * jnp.sum(fin[...], axis=0)
    dcap = jnp.concatenate(
        [dcap[q * caps : (q + 1) * caps, :] for q in range(packs)], axis=1
    )
    cg_ref[...] = cap_scale * (
        dcap - cap_unit * jnp.sum(cap_unit * dcap, axis=1, keepdims=True)
    )

    for i in range(n_chunks):
        mate_copy(i).wait_send()
        each(1, chips, lambda k: part_copy(k, i, chip_peer(k), chip).wait_send())
        each(1, chips, lambda k: dp_chip(k, i, chip).wait_send())
        each(0, chips, lambda c: dp_mate(i, c, core).wait_send())
    sum_copy.wait_send()
    each(1, shards, lambda k: cap_copy(k, t).wait_send())
    each(1, shards, lambda k: give_copy(k, shard_peer(k), t).wait_send())
    each(1, chips, lambda k: end_copy(k, chip).wait_send())


def solution(mesh):
    sections, shards = mesh.shape["section"], mesh.shape["shard"]
    chips = sections // 2

    def on_device(features, proj_weight, captions, positives):
        n_rows, depth = features.shape
        width = proj_weight.shape[1]
        caps = captions.shape[0]
        lanes = width * caps // SLOT
        n = CHUNKS
        rows = n_rows // sections // n
        half = chips * rows
        dma = pltpu.SemaphoreType.DMA
        any_space = pl.BlockSpec(memory_space=pl.ANY)
        vmem = pl.BlockSpec(memory_space=pltpu.VMEM)
        flops = 4 * n_rows * depth * width
        return pl.pallas_call(
            functools.partial(kernel, sections, shards),
            out_shape=(
                pltpu.VMEM((n_rows, depth), BF16), pltpu.VMEM((caps, width), F32)
            ),
            in_specs=[any_space, any_space, vmem, vmem],
            out_specs=(vmem, vmem),
            scratch_shapes=[
                pltpu.VMEM((n, 2, half, depth), BF16),
                pltpu.VMEM((depth, width), BF16),
                pltpu.VMEM((n, half, width), F32),
                pltpu.VMEM((n, half, width), BF16),
                pltpu.VMEM((n, half, width), BF16),
                pltpu.VMEM((n, chips, rows, width), BF16),
                pltpu.VMEM((chips, n, rows, width), BF16),
                pltpu.VMEM((n, 2, chips, rows, width), BF16),
                pltpu.VMEM((shards, SLOT, lanes), BF16),
                pltpu.VMEM((shards * SLOT, width), BF16),
                pltpu.VMEM((shards * SLOT, lanes), F32),
                pltpu.VMEM((shards * SLOT, lanes), F32),
                pltpu.VMEM((shards, SLOT, lanes), BF16),
                pltpu.VMEM((shards, SLOT, lanes), BF16),
                pltpu.VMEM((chips, SLOT, lanes), F32),
                dma((n, 2)), dma((PIECES,)),
                dma((n,)), dma((n,)),
                dma((chips, n)), dma((chips, n)),
                dma((chips, n)), dma((chips, n)),
                dma((chips, n)), dma((chips, n)),
                dma((shards,)), dma((shards,)),
                dma, dma,
                dma((shards,)), dma((shards,)),
                dma((chips,)), dma((chips,)),
            ],
            cost_estimate=pl.CostEstimate(
                flops=flops,
                bytes_accessed=2 * (2 * n_rows * depth + depth * width),
                transcendentals=0,
            ),
            compiler_params=pltpu.CompilerParams(
                collective_id=0, has_side_effects=True, vmem_limit_bytes=56 * 1024 * 1024
            ),
        )(features, proj_weight, captions, positives.reshape(1, n_rows))
    return jax.shard_map(
        on_device,
        mesh=mesh,
        in_specs=(P("shard", "section"), P("section", None), P("shard", None), P("shard")),
        out_specs=(P("shard", "section"), P("shard", None)),
        check_vma=False,
    )
```

```python
import functools

import jax
import jax.numpy as jnp
from jax import lax
from jax.experimental import pallas as pl
from jax.experimental.pallas import tpu as pltpu
from jax.sharding import PartitionSpec as P

logit_scale = 14.0
eps_norm = 1e-06
MESH = pl.DeviceIdType.MESH
F32 = jnp.float32
BF16 = jnp.bfloat16
SLOT = 16
CHUNKS = 2
PIECES = 3


def each(low, high, body):
    if high - low <= 8:
        for k in range(low, high):
            body(k)
    else:
        lax.fori_loop(low, high, lambda k, c: (body(k), c)[1], 0)


def kernel(
    sections, shards, f_hbm, w_hbm, cap_ref, pos_ref, rg_ref, cg_ref,
    fv, wv, own, psnd, prcv, xs, xr, dp, cs, tab, dacc, dpt, dsnd, drc, fin,
    f_sem, w_sem, ps_sem, pr_sem, xs_sem, xr_sem, ms_sem, mr_sem, ds_sem, dr_sem,
    cs_sem, cr_sem, as_sem, ar_sem, gs_sem, gr_sem, es_sem, er_sem,
):
    chips = sections // 2
    n_chunks, _, _, rows, width = dp.shape
    depth = wv.shape[0]
    half = chips * rows
    both = 2 * half
    caps = cap_ref.shape[0]
    packs = SLOT // caps
    lanes = width // packs
    sec = lax.axis_index("section")
    t = lax.axis_index("shard")
    core = lax.rem(sec, 2)
    chip = sec // 2
    mate = chip * 2 + (1 - core)

    def chip_peer(k):
        return lax.rem(chip + k, chips)

    def shard_peer(k):
        return lax.rem(t + k, shards)

    def place(c, s):
        return {"section": c, "shard": s}

    def to_mate(src, dst, send, recv):
        return pltpu.make_async_remote_copy(
            src_ref=src, dst_ref=dst, send_sem=send, recv_sem=recv,
            device_id=place(mate, t), device_id_type=MESH,
        )

    def to_chip(k, src, dst, send, recv):
        return pltpu.make_async_remote_copy(
            src_ref=src, dst_ref=dst, send_sem=send, recv_sem=recv,
            device_id=place(chip_peer(k) * 2 + core, t), device_id_type=MESH,
        )

    def to_shard(k, src, dst, send, recv):
        return pltpu.make_async_remote_copy(
            src_ref=src, dst_ref=dst, send_sem=send, recv_sem=recv,
            device_id=place(sec, shard_peer(k)), device_id_type=MESH,
        )

    step = depth // PIECES

    def f_copy(i, which):
        owner = core if which == 1 else 1 - core
        start = pl.multiple_of(i * both + owner * half, half)
        return pltpu.make_async_copy(
            f_hbm.at[pl.ds(start, half), :], fv.at[i, which], f_sem.at[i, which]
        )

    def w_copy(p):
        band = pl.ds(p * step, step)
        return pltpu.make_async_copy(w_hbm.at[band, :], wv.at[band, :], w_sem.at[p])

    for which in range(2):
        f_copy(0, which).start()
    for p in range(PIECES):
        w_copy(p).start()
    for i in range(1, n_chunks):
        for which in range(2):
            f_copy(i, which).start()

    barrier = pltpu.get_barrier_semaphore()

    def greet(c, s):
        pl.semaphore_signal(barrier, inc=1, device_id=place(c, s), device_id_type=MESH)

    greet(mate, t)
    each(1, chips, lambda k: greet(chip_peer(k) * 2 + core, t))
    each(1, shards, lambda k: greet(sec, shard_peer(k)))

    cap_float = cap_ref[...].astype(F32)
    cap_scale = lax.rsqrt(jnp.sum(cap_float * cap_float, axis=1, keepdims=True) + eps_norm)
    cap_unit = cap_float * cap_scale
    packed = jnp.concatenate(
        [cap_unit[:, q * lanes : (q + 1) * lanes] for q in range(packs)], axis=0
    )
    cs[t] = packed.astype(BF16)

    def cap_copy(k, source):
        return to_shard(k, cs.at[source], cs.at[source], cs_sem.at[k], cr_sem.at[source])

    def mate_copy(i):
        return to_mate(psnd.at[i], prcv.at[i], ps_sem.at[i], pr_sem.at[i])

    def part_copy(k, i, there, here):
        return to_chip(k, xs.at[i, there], xr.at[here, i], xs_sem.at[k, i], xr_sem.at[here, i])

    def chip_sum(i):
        mate_copy(i).wait_recv()
        value = own[i] + prcv[i].astype(F32)
        own[i] = value
        xs[i] = value.astype(BF16).reshape(chips, rows, width)
        each(1, chips, lambda k: part_copy(k, i, chip_peer(k), chip).start())

    for i in range(n_chunks):
        for which in range(2):
            f_copy(i, which).wait()
        part = None
        for p in range(PIECES):
            if i == 0:
                w_copy(p).wait()
            band = slice(p * step, (p + 1) * step)
            term = jnp.dot(
                fv[i, :, :, band].reshape(both, step), wv[band, :], preferred_element_type=F32
            )
            part = term if part is None else part + term
            if i >= 1 and p == PIECES - 2:
                chip_sum(i - 1)
        psnd[i] = part[:half].astype(BF16)
        own[i] = part[half:]
        if i == 0:
            pl.semaphore_wait(barrier, 1 + (chips - 1) + (shards - 1))
        mate_copy(i).start()
        if i == 0:
            each(1, shards, lambda k: cap_copy(k, t).start())
    chip_sum(n_chunks - 1)

    each(1, shards, lambda k: cap_copy(k, shard_peer(k)).wait_recv())
    per = min(8, shards)
    group = per * SLOT
    ra = lax.broadcasted_iota(jnp.int32, (group, group), 0)
    rb = lax.broadcasted_iota(jnp.int32, (group, group), 1)
    same = jnp.logical_and(ra // SLOT == rb // SLOT, ra % caps == rb % caps)
    picks = [
        jnp.logical_and(same, (rb % SLOT) // caps == q).astype(F32).astype(BF16)
        for q in range(packs)
    ]
    for g in range(shards // per):
        block = cs[g * per : (g + 1) * per].reshape(group, lanes)
        for q in range(packs):
            tab[g * group : (g + 1) * group, q * lanes : (q + 1) * lanes] = jnp.dot(
                picks[q], block, preferred_element_type=F32
            ).astype(BF16)

    positives = pos_ref[...]
    mine = core * chips + chip
    total = shards * SLOT
    ids = lax.broadcasted_iota(jnp.int32, (total, rows), 0)
    ids = caps * (ids // SLOT) + ids % caps
    piece = (lax.broadcasted_iota(jnp.int32, (total, lanes), 0) % SLOT) // caps

    def dp_chip(k, i, source):
        block = dp.at[i, core, source]
        return to_chip(k, block, block, ds_sem.at[k, i], dr_sem.at[source, i])

    def dp_mate(i, source, side):
        block = dp.at[i, side, source]
        return to_mate(block, block, ms_sem.at[source, i], mr_sem.at[source, i])

    sum_copy = to_mate(dacc, dpt, as_sem, ar_sem)

    def score(i):
        each(1, chips, lambda k: part_copy(k, i, chip_peer(k), chip_peer(k)).wait_recv())
        start = pl.multiple_of(chip * rows, rows)
        projected = own[i, pl.ds(start, rows), :]
        for k in range(1, chips):
            projected = projected + xr[chip_peer(k), i].astype(F32)
        scale = lax.rsqrt(jnp.sum(projected * projected, axis=1, keepdims=True) + eps_norm)
        unit = projected * scale
        unit_half = unit.astype(BF16)
        logits = logit_scale * lax.dot_general(
            tab[...], unit_half, (((1,), (1,)), ((), ())), preferred_element_type=F32
        )
        expon = jnp.exp(logits)
        probs = expon * (packs / jnp.sum(expon, axis=0, keepdims=True))
        index = positives[:, i * both : i * both + rows]
        for j in range(1, sections):
            low = i * both + j * rows
            index = jnp.where(mine == j, positives[:, low : low + rows], index)
        onehot = (ids == index).astype(F32)
        dlogits = (probs - onehot).astype(BF16)
        term = jnp.zeros((total, lanes), F32)
        for q in range(packs):
            value = jnp.dot(
                dlogits, unit_half[:, q * lanes : (q + 1) * lanes], preferred_element_type=F32
            )
            term = jnp.where(piece == q, value, term)
        dacc[...] = term if i == 0 else dacc[...] + term
        if i == n_chunks - 1:
            sum_copy.start()
        dunit = (logit_scale / packs) * lax.dot_general(
            dlogits, tab[...], (((0,), (0,)), ((), ())), preferred_element_type=F32
        )
        dproj = scale * (dunit - unit * jnp.sum(unit * dunit, axis=1, keepdims=True))
        dp[i, core, chip] = dproj.astype(BF16)
        each(1, chips, lambda k: dp_chip(k, i, chip).start())
        dp_mate(i, chip, core).start()

    def forward(i):
        def one(k):
            dp_chip(k, i, chip_peer(k)).wait_recv()
            dp_mate(i, chip_peer(k), core).start()

        each(1, chips, one)

    def grad(i, part, parts):
        if part == 0:
            each(0, chips, lambda c: dp_mate(i, c, 1 - core).wait_recv())
        size = depth // parts
        band = slice(part * size, (part + 1) * size)
        rg_ref[i * both : (i + 1) * both, band] = lax.dot_general(
            dp[i].reshape(both, width), wv[band, :], (((1,), (1,)), ((), ())),
            preferred_element_type=F32,
        ).astype(BF16)

    def give_copy(k, there, here):
        return to_shard(k, dsnd.at[there], drc.at[here], gs_sem.at[k], gr_sem.at[here])

    def end_copy(k, source):
        return to_chip(k, fin.at[source], fin.at[source], es_sem.at[k], er_sem.at[source])

    for i in range(n_chunks):
        score(i)
    forward(0)
    sum_copy.wait_recv()
    dsnd[...] = (dacc[...] + dpt[...]).astype(BF16).reshape(shards, SLOT, lanes)
    each(1, shards, lambda k: give_copy(k, shard_peer(k), t).start())
    drc[t] = dsnd[t]
    for i in range(n_chunks - 1):
        grad(i, 0, 1)
        forward(i + 1)
    grad(n_chunks - 1, 0, 2)
    each(1, shards, lambda k: give_copy(k, shard_peer(k), shard_peer(k)).wait_recv())
    fin[chip] = jnp.sum(drc[...].astype(F32), axis=0)
    each(1, chips, lambda k: end_copy(k, chip).start())
    grad(n_chunks - 1, 1, 2)
    each(1, chips, lambda k: end_copy(k, chip_peer(k)).wait_recv())
    dcap = logit_scale * jnp.sum(fin[...], axis=0)
    dcap = jnp.concatenate(
        [dcap[q * caps : (q + 1) * caps, :] for q in range(packs)], axis=1
    )
    cg_ref[...] = cap_scale * (
        dcap - cap_unit * jnp.sum(cap_unit * dcap, axis=1, keepdims=True)
    )

    for i in range(n_chunks):
        mate_copy(i).wait_send()
        each(1, chips, lambda k: part_copy(k, i, chip_peer(k), chip).wait_send())
        each(1, chips, lambda k: dp_chip(k, i, chip).wait_send())
        each(0, chips, lambda c: dp_mate(i, c, core).wait_send())
    sum_copy.wait_send()
    each(1, shards, lambda k: cap_copy(k, t).wait_send())
    each(1, shards, lambda k: give_copy(k, shard_peer(k), t).wait_send())
    each(1, chips, lambda k: end_copy(k, chip).wait_send())


def solution(mesh):
    sections, shards = mesh.shape["section"], mesh.shape["shard"]
    chips = sections // 2

    def on_device(features, proj_weight, captions, positives):
        n_rows, depth = features.shape
        width = proj_weight.shape[1]
        caps = captions.shape[0]
        lanes = width * caps // SLOT
        n = CHUNKS
        rows = n_rows // sections // n
        half = chips * rows
        dma = pltpu.SemaphoreType.DMA
        any_space = pl.BlockSpec(memory_space=pl.ANY)
        vmem = pl.BlockSpec(memory_space=pltpu.VMEM)
        flops = 4 * n_rows * depth * width
        return pl.pallas_call(
            functools.partial(kernel, sections, shards),
            out_shape=(
                pltpu.VMEM((n_rows, depth), BF16), pltpu.VMEM((caps, width), F32)
            ),
            in_specs=[any_space, any_space, vmem, vmem],
            out_specs=(vmem, vmem),
            scratch_shapes=[
                pltpu.VMEM((n, 2, half, depth), BF16),
                pltpu.VMEM((depth, width), BF16),
                pltpu.VMEM((n, half, width), F32),
                pltpu.VMEM((n, half, width), BF16),
                pltpu.VMEM((n, half, width), BF16),
                pltpu.VMEM((n, chips, rows, width), BF16),
                pltpu.VMEM((chips, n, rows, width), BF16),
                pltpu.VMEM((n, 2, chips, rows, width), BF16),
                pltpu.VMEM((shards, SLOT, lanes), BF16),
                pltpu.VMEM((shards * SLOT, width), BF16),
                pltpu.VMEM((shards * SLOT, lanes), F32),
                pltpu.VMEM((shards * SLOT, lanes), F32),
                pltpu.VMEM((shards, SLOT, lanes), BF16),
                pltpu.VMEM((shards, SLOT, lanes), BF16),
                pltpu.VMEM((chips, SLOT, lanes), F32),
                dma((n, 2)), dma((PIECES,)),
                dma((n,)), dma((n,)),
                dma((chips, n)), dma((chips, n)),
                dma((chips, n)), dma((chips, n)),
                dma((chips, n)), dma((chips, n)),
                dma((shards,)), dma((shards,)),
                dma, dma,
                dma((shards,)), dma((shards,)),
                dma((chips,)), dma((chips,)),
            ],
            cost_estimate=pl.CostEstimate(
                flops=flops,
                bytes_accessed=2 * (2 * n_rows * depth + depth * width),
                transcendentals=0,
            ),
            compiler_params=pltpu.CompilerParams(
                collective_id=0, has_side_effects=True, vmem_limit_bytes=56 * 1024 * 1024
            ),
        )(features, proj_weight, captions, positives.reshape(1, n_rows))
    return jax.shard_map(
        on_device,
        mesh=mesh,
        in_specs=(P("shard", "section"), P("section", None), P("shard", None), P("shard")),
        out_specs=(P("shard", "section"), P("shard", None)),
        check_vma=False,
    )
```
